128 devices in a mesh: dp: 8 (over z_hi, x), expert: 16 (over z_lo, y, core).
Axes of the slice: x: 4, y: 4, z: 4 (z_hi: 2, z_lo: 2; z = z_hi * 2 + z_lo), core: 2. Of those that a mesh axis runs over, the one named last changes fastest.
Arguments:
- frames: bfloat16 [8, 2048, 1536], P('dp', 'expert'), may hold values from -6 to 6
- lengths: int32 [8], P('dp'), may hold values from 1024 to 2048, as said below
- kernel: float32 [31, 1536], replicated, may hold values from -1 to 1
- expert_ids: int32 [8, 2048, 2], P('dp', 'expert'), may hold values from 0 to 15, all different within a row; in each aligned block of 128 rows (0 to 127, 128 to 255, ..., all dimensions but the last counted through in order) at most 18 rows name the same one
- gate_weights: float32 [8, 2048, 2], P('dp', 'expert'), may hold values from 0.1 to 0.9
- w_in: bfloat16 [16, 1536, 6144], P('expert', None, 'dp'), may hold values from -0.15625 to 0.15625
- w_out: bfloat16 [16, 6144, 1536], P('expert', 'dp'), may hold values from -0.078125 to 0.078125
- cotangent: bfloat16 [8, 2048, 1536], P('dp', 'expert'), may hold values from -6 to 6
Outputs:
- grad_frames: bfloat16 [8, 2048, 1536], P('dp', 'expert')
- grad_kernel: float32 [31, 1536], P(None, ('dp', 'expert'))
- grad_w_in: float32 [16, 1536, 6144], P('expert', None, 'dp')
- grad_w_out: float32 [16, 6144, 1536], P('expert', 'dp')
The draws below stay inside these ranges and needn't reach their ends.
Inputs may be any that keep to these rules, and one draw needn't show every extreme that they name: `lengths`: valid frames of each utterance; at least one utterance has all 2048. `expert_ids`: each frame names two different experts; among the 128 frames of one index of expert in one utterance no expert is named more than 18 times, a bound that some block reaches.
All inputs are finite; a program needn't handle non-finite values.
Results may differ from the reference program's by a relative error of at most 0.006.
Values may be sent and summed in bfloat16 or wider, within the bound.
No kernel may reach another device: no remote copies, remote signals or barrier semaphores. Data moves between devices by JAX's collectives and lax.ppermute only.
A program may use at most 192 MiB of HBM per device.

```python
import math
import jax
import jax.numpy as jnp
import numpy as np
from jax import lax

D = 1536
FF = 6144
KW = 31
BLK = 128
EXPERTS = 16
UTT = 8
LEN = 2048
MOST = 18
N_EXPERT = 16


def draw_lengths(key, part):
    key = jax.random.fold_in(key, 7)
    first_key, second_key = jax.random.split(key)
    values = jax.random.randint(first_key, (UTT,), LEN // 2, LEN + 1)
    picked = jax.random.randint(second_key, (), 0, UTT)
    return jnp.where(jnp.arange(UTT) == picked, LEN, values).astype(jnp.int32)


def strengthened(array, key, source, target, parts, factor):
    def block_of(axis_at):
        return (jnp.arange(array.shape[axis_at]) // (array.shape[axis_at] // parts)).reshape((-1,) + (1,) * (array.ndim - 1 - axis_at))

    near = jax.random.permutation(key, parts)[block_of(target)]
    second = (block_of(target) + parts // 2) % parts
    return jnp.where((block_of(source) == near) | (block_of(source) == second), factor * array, array)


def levels(own_key, shape, cuts, low, high):
    def one(dim, shards_of):
        steps = jax.random.uniform(jax.random.fold_in(jax.random.fold_in(own_key, 6), dim), (shards_of,), jnp.float32, low / len(cuts), high / len(cuts))
        return jnp.repeat(jnp.exp(steps), shape[dim] // shards_of).reshape((-1,) + (1,) * (len(shape) - dim - 1))

    level = one(*cuts[0])
    for cut in cuts[1:]:
        level = level * one(*cut)
    return level


def deal_out(rng, own, number, rows, number_of, top, reach, lean):
    ranking = jax.random.permutation(rng, number_of)
    crowded, common = shares(number_of, rows * top, reach, lean, True), shares(number_of, rows * top, reach, lean, False)
    places = jnp.arange(number_of)

    def named(sizes, offset_by):
        used = int((sizes > 0).sum())
        fixed = max(1, used // 4)
        moved = fixed + (places - fixed + offset_by * (used - fixed)) % max(1, number_of - fixed)
        return jnp.zeros((number_of,), jnp.int32).at[ranking[jnp.where(places < fixed, places, moved)]].set(jnp.asarray(sizes, jnp.int32))

    sizes = jnp.where(number % 4 == 0, named(crowded, number // 4), named(common, number - number // 4 - 1))
    mixed = jax.random.permutation(jax.random.fold_in(own, 3), number_of)
    source_of, taker = mixed[0:number_of // 2 * 2:2], mixed[1:number_of // 2 * 2:2]
    room = jnp.minimum(sizes[source_of] - 1, reach - sizes[taker]) // 2
    room = jnp.where((source_of == ranking[0]) | (taker == ranking[0]) | (sizes[taker] == 0), 0, jnp.maximum(room, 0))
    moved = jax.random.randint(jax.random.fold_in(own, 4), (number_of // 2,), 0, 1 << 20) % (room + 1)
    sizes = sizes.at[source_of].add(-moved).at[taker].add(moved)
    labels = jnp.searchsorted(jnp.cumsum(sizes), jnp.arange(rows * top), side="right").astype(jnp.int32)
    listing = labels.reshape(top, rows).T
    listing = listing[jax.random.permutation(jax.random.fold_in(own, 1), rows)]
    offset_by = jax.random.randint(jax.random.fold_in(own, 2), (rows, 1), 0, top)
    return jnp.take_along_axis(listing, (jnp.arange(top)[None, :] + offset_by) % top, axis=1)


def shares(count, total, most, lean, full):
    loads = [(1 << 20) // math.isqrt(rank ** lean) + 1 for rank in range(1, count + 1)]
    largest = most if full else min(most, max(-(-total // count), total * loads[0] // sum(loads)))
    least = 1 if total - largest >= count - 1 else 0
    holding, surplus = [largest] + [least] * (count - 1), total - largest - least * (count - 1)
    while surplus > 0:
        movable = [i for i in range(1, count) if holding[i] < largest] or [i for i in range(1, count) if holding[i] < most]
        pool, budget = sum([loads[i] for i in movable]), surplus
        for i in movable:
            extra = min(most - holding[i], max(1, budget * loads[i] // pool), surplus)
            holding[i] = holding[i] + extra
            surplus = surplus - extra
    return np.array(holding)


def bell_draw(key, dims, spread, most, shards=(), held_as=jnp.bfloat16):
    loudness = levels(key, dims, shards, -0.22, 0.18) if shards else 1.0
    array = jax.random.normal(key, dims, jnp.float32) * spread * loudness
    return jnp.minimum(jnp.maximum(array, -most), most).astype(held_as)


def bell_draw_with(stream_key, extent, deviation, reach, shards, heavy, kind=jnp.bfloat16):
    values = deviation * jax.random.normal(stream_key, extent, jnp.float32)
    if shards:
        values = values * levels(stream_key, extent, shards, -0.22, 0.18)
    return jnp.clip(strengthened(values, jax.random.fold_in(stream_key, 3), *heavy), -reach, reach).astype(kind)


def setup_inputs(seed: int = 0) -> dict:
    splits = jax.random.split(jax.random.key(seed), 9)
    frames = bell_draw(splits[0], (UTT, LEN, D), 1.0, 6.0, ((0, 8), (1, 16)))
    lengths = draw_lengths(jax.random.fold_in(splits[8], 71), 0)
    kernel = bell_draw(splits[2], (KW, D), KW ** -0.5, 1.0, (), jnp.float32)
    expert_ids_keys = jax.random.split(jax.random.fold_in(splits[3], 1), UTT * LEN // BLK)
    expert_ids_turns = jax.random.permutation(jax.random.fold_in(splits[3], 3), UTT * LEN // BLK)
    expert_ids = jax.vmap(lambda own, number: deal_out(jax.random.fold_in(splits[3], 2), own, number, BLK, EXPERTS, 2, MOST, 1))(expert_ids_keys, expert_ids_turns).reshape((UTT, LEN, 2))
    gate_weights = jnp.clip(0.1 + 0.79999997 * jax.random.uniform(splits[4], (UTT, LEN, 2), jnp.float32) ** levels(splits[4], (UTT, LEN, 2), ((0, 8), (1, 16)), -0.2, 0.2), 0.1, 0.9)
    w_in = bell_draw(splits[5], (EXPERTS, D, FF), D ** -0.5, 0.15625, ((0, 16), (2, 8)))
    w_out = bell_draw(splits[6], (EXPERTS, FF, D), FF ** -0.5, 0.078125, ((0, 16), (1, 8)))
    cotangent = bell_draw_with(splits[7], (UTT, LEN, D), 1.0, 6.0, ((0, 8), (1, 16)), (1, 2, 16, 2.0))
    return {"frames": frames, "lengths": lengths, "kernel": kernel, "expert_ids": expert_ids, "gate_weights": gate_weights, "w_in": w_in, "w_out": w_out, "cotangent": cotangent}


EPSILON = 1e-06

def rms_scale(values):
    return values * lax.rsqrt(lax.optimization_barrier(jnp.mean(values * values, axis=-1, keepdims=True)) + EPSILON)

def reference(frames, lengths, kernel, expert_ids, gate_weights, w_in, w_out, cotangent):
    utt_count, seq_len, model_width = frames.shape
    half_width = KW // 2
    positions = jnp.arange(seq_len, dtype=jnp.int32)
    frame_mask = (positions[None, :] < lengths[:, None]).astype(jnp.float32)
    masked = (frames.astype(jnp.float32) * frame_mask[..., None]).astype(jnp.bfloat16)
    padded = jnp.pad(masked, ((0, 0), (half_width, half_width), (0, 0)))
    conv = jnp.zeros((utt_count, seq_len, model_width), jnp.float32)
    for tap in range(KW):
        conv = conv + kernel[tap] * padded[:, tap:tap + seq_len].astype(jnp.float32)
    resid = frames.astype(jnp.float32) + conv
    normed_exact, norm_back = jax.vjp(rms_scale, resid)
    normed = normed_exact.astype(jnp.bfloat16)
    coeff = 0.5 * gate_weights * frame_mask[..., None]
    expert_cot = (coeff[..., None] * cotangent.astype(jnp.float32)[:, :, None, :]).astype(jnp.bfloat16)
    route_total = utt_count * seq_len * 2
    expert_cot = expert_cot.reshape(route_total, model_width)
    flat_normed = normed.reshape(utt_count * seq_len, model_width)
    route_ids = expert_ids.reshape(route_total)
    limit = UTT * N_EXPERT * MOST

    def per_expert(carry, expert):
        chosen = jnp.nonzero(route_ids == expert, size=limit, fill_value=0)[0].astype(jnp.int32)
        count = jnp.sum((route_ids == expert).astype(jnp.int32))
        usable = jnp.arange(limit, dtype=jnp.int32) < count
        rows_n = flat_normed[chosen // 2]
        rows_g = jnp.where(usable[:, None], expert_cot[chosen], jnp.zeros((), jnp.bfloat16)).astype(jnp.bfloat16)
        weight_in = lax.dynamic_index_in_dim(w_in, expert, 0, keepdims=False)
        weight_out = lax.dynamic_index_in_dim(w_out, expert, 0, keepdims=False)
        pre_act = jnp.dot(rows_n, weight_in, preferred_element_type=jnp.float32)
        hidden = jax.nn.silu(pre_act).astype(jnp.bfloat16)
        hidden_cot = jnp.dot(rows_g, weight_out.T, preferred_element_type=jnp.float32)
        sigmoid_pre = jax.nn.sigmoid(pre_act)
        pre_cot = (hidden_cot * sigmoid_pre * (1.0 + pre_act * (1.0 - sigmoid_pre))).astype(jnp.bfloat16)
        grad_out = jnp.dot(hidden.T, rows_g, preferred_element_type=jnp.float32)
        grad_in = jnp.dot(rows_n.T, pre_cot, preferred_element_type=jnp.float32)
        route_cot = jnp.dot(pre_cot, weight_in.T, preferred_element_type=jnp.float32).astype(jnp.bfloat16)
        route_cot = lax.optimization_barrier(route_cot).astype(jnp.float32)
        carry = carry.at[chosen].add(jnp.where(usable[:, None], route_cot, jnp.zeros((), jnp.float32)))
        return (carry, (grad_in, grad_out))
    start = jnp.zeros((route_total, model_width), jnp.float32)
    routes_cot, (grad_w_in, grad_w_out) = lax.scan(per_expert, start, jnp.arange(EXPERTS, dtype=jnp.int32))
    normed_cot = routes_cot.reshape(utt_count, seq_len, 2, model_width).sum(axis=2)
    resid_cot = cotangent.astype(jnp.float32) + norm_back(normed_cot)[0]
    kernel_rows = []
    for tap in range(KW):
        kernel_rows.append(lax.optimization_barrier(jnp.sum(resid_cot * padded[:, tap:tap + seq_len].astype(jnp.float32), axis=(0, 1))))
    grad_kernel = jnp.stack(kernel_rows, axis=0)
    grad_pad = jnp.pad(resid_cot, ((0, 0), (half_width, half_width), (0, 0)))
    spread_back = jnp.zeros((utt_count, seq_len, model_width), jnp.float32)
    for tap in range(KW):
        offset = 2 * half_width - tap
        spread_back = spread_back + kernel[tap] * grad_pad[:, offset:offset + seq_len]
    grad_frames = (resid_cot + frame_mask[..., None] * spread_back).astype(jnp.bfloat16)
    return (grad_frames, grad_kernel, grad_w_in, grad_w_out)
```

```python
import jax
import jax.numpy as jnp
from jax import lax
from jax.experimental import pallas as pl
from jax.experimental.pallas import tpu as pltpu
from jax.sharding import PartitionSpec as P

EPSILON = 1e-06
AXES = ("dp", "expert")
SLOTS = 18
X, Y, Z = 4, 4, 4


def number_of(x, y, z, core):
    return ((z // 2) * X + x) * 16 + (z % 2) * 8 + y * 2 + core


def moved(rows, dx=0, dy=0, dz=0, dc=0):
    pairs = []
    for x in range(X):
        for y in range(Y):
            for z in range(Z):
                for core in range(2):
                    pairs.append(
                        (
                            number_of(x, y, z, core),
                            number_of((x + dx) % X, (y + dy) % Y, (z + dz) % Z, core ^ dc),
                        )
                    )
    return lax.ppermute(rows, AXES, pairs)


def extended(cells, width):
    count = lax.axis_size("expert")
    ends = count - 1
    head = cells[:width]
    tail = cells[-width:]
    return jnp.concatenate(
        [
            lax.ppermute(tail, "expert", [(i, i + 1) for i in range(ends)]),
            cells,
            lax.ppermute(head, "expert", [(i + 1, i) for i in range(ends)]),
        ],
        axis=0,
    )


def rms_scale(values):
    return values * lax.rsqrt(jnp.mean(values * values, axis=-1, keepdims=True) + EPSILON)


def dot(a, b, ca, cb, kind=jnp.float32):
    return lax.dot_general(
        a, b, (((ca,), (cb,)), ((), ())), preferred_element_type=jnp.float32
    ).astype(kind)


def order():
    place = jnp.arange(16 * SLOTS, dtype=jnp.int32)
    slot = place % SLOTS
    source = (place // SLOTS) % 4
    rz = (place // (4 * SLOTS)) % 2
    rc = place // (8 * SLOTS)
    taken = source * 4 * SLOTS + rz * 2 * SLOTS + rc * SLOTS + slot
    return (taken[:, None] == place[None, :]).astype(jnp.bfloat16)


X_GROUPS = [[0, 1, 2, 3], [4, 5, 6, 7]]


def after(value, *earlier):
    return lax.optimization_barrier((value, *earlier))[0]


def together(*values):
    return lax.optimization_barrier(values)


def along_y(rows):
    part = 4 * SLOTS
    pieces = [rows[part * r : part * r + part] for r in range(4)]
    return pieces[:1] + [moved(pieces[r], dy=r) for r in range(1, 4)]


def to_cores(pieces, arrange):
    part = 4 * SLOTS
    placed = dot(arrange, jnp.concatenate(pieces, axis=0), 1, 0, jnp.bfloat16)
    core = moved(placed[2 * part :], dc=1)
    same = jnp.concatenate([placed[:part], core[:part]], axis=0)
    other = jnp.concatenate([placed[part : 2 * part], core[part:]], axis=0)
    return same, other


def neighbours(same, other):
    return moved(other, dz=1), moved(other, dz=-1), moved(same, dx=1), moved(same, dx=-1)


def gathered(up, down):
    other = jnp.concatenate([up, down], axis=0)
    return lax.all_gather(other, "dp", axis=0, tiled=True, axis_index_groups=X_GROUPS)


def total(*terms):
    out = terms[0].astype(jnp.float32)
    for term in terms[1:]:
        out = out + term.astype(jnp.float32)
    return out.astype(jnp.bfloat16)


def sent_back(first, other, second, arrange, grad_in, grad_out):
    part = 4 * SLOTS
    first = total(first[: 4 * part], after(moved(first[4 * part :], dz=2), other))
    second_from = moved(second[4 * part :], dz=2)
    second = total(second[: 4 * part], second_from)
    s1, s3, s2 = moved(first[2 * part :], dx=-1), moved(second[: 2 * part], dx=1), moved(
        second[2 * part :], dx=2
    )
    same = total(first[: 2 * part], s1, s3, s2)
    other = lax.psum_scatter(
        other, "dp", scatter_dimension=0, tiled=True, axis_index_groups=X_GROUPS
    )
    other = total(moved(other[: 2 * part], dz=-1), moved(other[2 * part :], dz=1))
    same, other, grad_in, grad_out = together(same, other, grad_in, grad_out)
    core = moved(jnp.concatenate([same[part:], other[part:]], axis=0), dc=1)
    placed = jnp.concatenate([same[:part], other[:part], core], axis=0)
    rows = dot(arrange, placed, 0, 0, jnp.bfloat16)
    pieces = [rows[part * r : part * r + part] for r in range(4)]
    pieces = pieces[:1] + [moved(pieces[r], dy=-r) for r in range(1, 4)]
    return jnp.concatenate(pieces, axis=0), grad_in, grad_out


def tap_sums_kernel(resid_cot, rim, out, wide, sums):
    rows, width = resid_cot.shape
    wide[...] = rim[...].astype(jnp.float32)
    sums[...] = jnp.zeros_like(sums)

    @pl.loop(0, width // 128)
    def _(tile):
        lanes = pl.ds(pl.multiple_of(tile * 128, 128), 128)
        cot = resid_cot[:, lanes]
        for tap in range(31):
            product = cot * wide[pl.ds(tap, rows), lanes]
            sums[pl.ds(tap, 1), lanes] = jnp.sum(product, axis=0, keepdims=True)

    share = width // 8
    for part in range(8):
        low = part * share // 128 * 128
        high = min(low + 384, width)
        piece = sums[:, low:high]
        shift = part * share - low
        if shift:
            piece = pltpu.roll(piece, high - low - shift, 1)
        out[part] = piece[:, :256]


def tap_sums(resid_cot, rim):
    width = resid_cot.shape[1]
    return pl.pallas_call(
        tap_sums_kernel,
        out_shape=jax.ShapeDtypeStruct((8, 32, 256), jnp.float32),
        scratch_shapes=[
            pltpu.VMEM(rim.shape, jnp.float32),
            pltpu.VMEM((32, width), jnp.float32),
        ],
        compiler_params=pltpu.CompilerParams(vmem_limit_bytes=16 * 2**20),
        name="tap_sums",
    )(resid_cot, rim)


def split_columns_kernel(share, parts, out):
    whole = parts[0]
    for part in range(1, 8):
        whole = whole + parts[part]
    whole = jnp.concatenate([whole, jnp.zeros((32, 128), jnp.float32)], axis=1)
    for part in range(16):
        piece = pltpu.roll(whole, 384 - share * part, 1) if part else whole
        out[part] = piece[:, :128]


def split_columns(parts, share):
    return pl.pallas_call(
        lambda *refs: split_columns_kernel(share, *refs),
        out_shape=jax.ShapeDtypeStruct((16, 32, 128), jnp.float32),
        compiler_params=pltpu.CompilerParams(vmem_limit_bytes=16 * 2**20),
        name="split_columns",
    )(parts)


def local(frames, lengths, kernel, expert_ids, gate_weights, w_in, w_out, cotangent):
    block_len = frames.shape[1]
    model_width = frames.shape[2]
    tap_count = kernel.shape[0]
    half_width = tap_count // 2
    place = lax.axis_index("expert")
    my_z, my_y, my_core = place // 8, (place // 2) % 4, place % 2
    positions = place * block_len + jnp.arange(block_len, dtype=jnp.int32)
    frame_mask = (positions < lengths[0]).astype(jnp.float32)
    arrange = order()

    ids = expert_ids[0]
    experts = jnp.arange(16, dtype=jnp.int32)
    named = (ids[:, :, None] == experts).astype(jnp.float32)
    both = named[:, 0] + named[:, 1]
    earlier = jnp.cumsum(both, axis=0) - both
    base = (
        ((experts // 2 - my_y) % 4) * 72
        + (experts // 8 != my_z) * 36
        + (experts % 2 != my_core) * 18
    ).astype(jnp.float32)
    target = jnp.sum(named * (earlier + base)[:, None, :], axis=2).astype(jnp.int32)
    rows = jnp.arange(16 * SLOTS, dtype=jnp.int32)
    hit = rows[:, None, None] == target[None]
    frame_place = jnp.any(hit, axis=2).astype(jnp.bfloat16)
    coeff = 0.5 * gate_weights[0] * frame_mask[:, None]
    row_coeff = jnp.sum(jnp.where(hit, coeff[None], 0.0), axis=(1, 2))

    cot_rows = (row_coeff[:, None] * dot(frame_place, cotangent[0], 1, 0)).astype(jnp.bfloat16)
    masked = (frames[0].astype(jnp.float32) * frame_mask[:, None]).astype(jnp.bfloat16)
    frame_rim = extended(masked, half_width)
    rim = jnp.concatenate([frame_rim, jnp.zeros((2, model_width), jnp.bfloat16)], axis=0)
    conv = jnp.zeros((block_len, model_width), jnp.float32)
    for tap in range(tap_count):
        conv = conv + kernel[tap] * frame_rim[tap : tap + block_len].astype(jnp.float32)
    resid = frames[0].astype(jnp.float32) + conv
    normed_exact, norm_back = jax.vjp(rms_scale, resid)
    normed = normed_exact.astype(jnp.bfloat16)
    normed_rows = dot(frame_place, normed, 1, 0, jnp.bfloat16)

    y_cot = along_y(cot_rows)
    *y_cot, normed_rows = together(*y_cot, normed_rows)
    same_cot, other_cot, *y_normed = together(*to_cores(y_cot, arrange), *along_y(normed_rows))
    up, down, s1, s3 = together(*neighbours(same_cot, other_cot))
    gathered_cot = gathered(up, down)
    same, other = to_cores(y_normed, arrange)
    same, other = after(same, s1), after(other, s1)
    first_cot = jnp.concatenate([same_cot, s1], axis=0)
    up, down, s2, first_far, same = together(
        moved(other, dz=1),
        moved(other, dz=-1),
        moved(same_cot, dx=2),
        moved(first_cot, dz=2),
        same,
    )
    other_normed = gathered(after(up, gathered_cot), down)
    second_cot = jnp.concatenate([s3, s2], axis=0)
    first_cot = jnp.concatenate([first_cot, first_far], axis=0)
    second_far, s1, s3 = together(
        moved(second_cot, dz=2), moved(same, dx=1), moved(same, dx=-1)
    )
    second_cot = jnp.concatenate([second_cot, second_far], axis=0)
    first_normed = jnp.concatenate([same, s1], axis=0)
    first_far, s2 = together(moved(first_normed, dz=2), moved(same, dx=2))
    second_normed = jnp.concatenate([s3, s2], axis=0)
    second_far = moved(second_normed, dz=2)
    first_normed = jnp.concatenate([first_normed, first_far], axis=0)

    weight_in = w_in[0]
    weight_out = w_out[0]
    partials = []
    hiddens = []
    pre_cots = []
    for rows_cot, rows_normed in (
        (first_cot, first_normed),
        (gathered_cot, other_normed),
        (second_cot, second_normed),
    ):
        if partials:
            rows_normed = after(rows_normed, partials[-1])
        if rows_normed.shape != rows_cot.shape:
            rows_normed = jnp.concatenate([rows_normed, after(second_far, partials[-1])], axis=0)
            second_normed = rows_normed
        hidden_cot = dot(rows_cot, weight_out, 1, 1)
        pre_act = dot(rows_normed, weight_in, 1, 0)
        sigmoid_pre = jax.nn.sigmoid(pre_act)
        hiddens.append((pre_act * sigmoid_pre).astype(jnp.bfloat16))
        pre_cot = (hidden_cot * sigmoid_pre * (1.0 + pre_act * (1.0 - sigmoid_pre))).astype(
            jnp.bfloat16
        )
        pre_cots.append(pre_cot)
        partials.append(dot(pre_cot, weight_in, 1, 1, jnp.bfloat16))
    cots = jnp.concatenate([first_cot, gathered_cot, second_cot], axis=0)
    normeds = jnp.concatenate([first_normed, other_normed, second_normed], axis=0)
    grad_out = dot(jnp.concatenate(hiddens, axis=0), cots, 0, 0)
    grad_in = dot(normeds, jnp.concatenate(pre_cots, axis=0), 0, 0)
    returned, grad_in, grad_out = sent_back(*partials, arrange, grad_in, grad_out)
    normed_cot = dot(frame_place, returned, 0, 0)

    resid_cot = cotangent[0].astype(jnp.float32) + norm_back(normed_cot)[0]
    taps = tap_sums(resid_cot, rim)
    taps = split_columns(lax.all_to_all(taps, "dp", 0, 0, tiled=True), model_width // 128)
    taps = lax.all_to_all(taps, "expert", 0, 0, tiled=True)
    grad_kernel = taps[:, :tap_count, : model_width // 128].sum(axis=0)
    grad_rim = extended(resid_cot, half_width)
    spread_back = jnp.zeros((block_len, model_width), jnp.float32)
    for tap in range(tap_count):
        offset = 2 * half_width - tap
        spread_back = spread_back + kernel[tap] * grad_rim[offset : offset + block_len]
    grad_frames = (resid_cot + frame_mask[:, None] * spread_back).astype(jnp.bfloat16)
    return (grad_frames[None], grad_kernel, grad_in[None], grad_out[None])


def solution(mesh):
    return jax.shard_map(
        local,
        mesh=mesh,
        in_specs=(
            P("dp", "expert", None),
            P("dp"),
            P(),
            P("dp", "expert", None),
            P("dp", "expert", None),
            P("expert", None, "dp"),
            P("expert", "dp", None),
            P("dp", "expert", None),
        ),
        out_specs=(
            P("dp", "expert", None),
            P(None, ("dp", "expert")),
            P("expert", None, "dp"),
            P("expert", "dp", None),
        ),
        check_vma=False,
    )
```

```python
import jax
import jax.numpy as jnp
from jax import lax
from jax.experimental import pallas as pl
from jax.experimental.pallas import tpu as pltpu
from jax.sharding import PartitionSpec as P

EPSILON = 1e-06
AXES = ("dp", "expert")
SLOTS = 18
X, Y, Z = 4, 4, 4


def number_of(x, y, z, core):
    return ((z // 2) * X + x) * 16 + (z % 2) * 8 + y * 2 + core


def moved(rows, dx=0, dy=0, dz=0, dc=0):
    pairs = []
    for x in range(X):
        for y in range(Y):
            for z in range(Z):
                for core in range(2):
                    pairs.append(
                        (
                            number_of(x, y, z, core),
                            number_of((x + dx) % X, (y + dy) % Y, (z + dz) % Z, core ^ dc),
                        )
                    )
    return lax.ppermute(rows, AXES, pairs)


def extended(cells, width):
    count = lax.axis_size("expert")
    ends = count - 1
    head = cells[:width]
    tail = cells[-width:]
    return jnp.concatenate(
        [
            lax.ppermute(tail, "expert", [(i, i + 1) for i in range(ends)]),
            cells,
            lax.ppermute(head, "expert", [(i + 1, i) for i in range(ends)]),
        ],
        axis=0,
    )


def rms_scale(values):
    return values * lax.rsqrt(jnp.mean(values * values, axis=-1, keepdims=True) + EPSILON)


def dot(a, b, ca, cb, kind=jnp.float32):
    return lax.dot_general(
        a, b, (((ca,), (cb,)), ((), ())), preferred_element_type=jnp.float32
    ).astype(kind)


def order():
    place = jnp.arange(16 * SLOTS, dtype=jnp.int32)
    slot = place % SLOTS
    source = (place // SLOTS) % 4
    rz = (place // (4 * SLOTS)) % 2
    rc = place // (8 * SLOTS)
    taken = source * 4 * SLOTS + rz * 2 * SLOTS + rc * SLOTS + slot
    return (taken[:, None] == place[None, :]).astype(jnp.bfloat16)


X_GROUPS = [[0, 1, 2, 3], [4, 5, 6, 7]]


def after(value, *earlier):
    return lax.optimization_barrier((value, *earlier))[0]


def together(*values):
    return lax.optimization_barrier(values)


def along_y(rows):
    part = 4 * SLOTS
    pieces = [rows[part * r : part * r + part] for r in range(4)]
    return pieces[:1] + [moved(pieces[r], dy=r) for r in range(1, 4)]


def to_cores(pieces, arrange):
    part = 4 * SLOTS
    placed = dot(arrange, jnp.concatenate(pieces, axis=0), 1, 0, jnp.bfloat16)
    core = moved(placed[2 * part :], dc=1)
    same = jnp.concatenate([placed[:part], core[:part]], axis=0)
    other = jnp.concatenate([placed[part : 2 * part], core[part:]], axis=0)
    return same, other


def neighbours(same, other):
    return moved(other, dz=1), moved(other, dz=-1), moved(same, dx=1), moved(same, dx=-1)


def gathered(up, down):
    other = jnp.concatenate([up, down], axis=0)
    return lax.all_gather(other, "dp", axis=0, tiled=True, axis_index_groups=X_GROUPS)


def total(*terms):
    out = terms[0].astype(jnp.float32)
    for term in terms[1:]:
        out = out + term.astype(jnp.float32)
    return out.astype(jnp.bfloat16)


def sent_back(first, other, second, arrange, grad_in, grad_out):
    part = 4 * SLOTS
    same = total(
        second[: 2 * part],
        moved(first[: 2 * part], dx=-1),
        moved(first[2 * part :], dx=1),
        moved(second[2 * part :], dx=2),
    )
    other = total(moved(other[: 2 * part], dz=-1), moved(other[2 * part :], dz=1))
    same, other, grad_in, grad_out = together(same, other, grad_in, grad_out)
    core = moved(jnp.concatenate([same[part:], other[part:]], axis=0), dc=1)
    placed = jnp.concatenate([same[:part], other[:part], core], axis=0)
    rows = dot(arrange, placed, 0, 0, jnp.bfloat16)
    pieces = [rows[part * r : part * r + part] for r in range(4)]
    pieces = pieces[:1] + [moved(pieces[r], dy=-r) for r in range(1, 4)]
    return jnp.concatenate(pieces, axis=0), grad_in, grad_out


def tap_sums_kernel(resid_cot, rim, out, wide, sums):
    rows, width = resid_cot.shape
    wide[...] = rim[...].astype(jnp.float32)
    sums[...] = jnp.zeros_like(sums)

    @pl.loop(0, width // 128)
    def _(tile):
        lanes = pl.ds(pl.multiple_of(tile * 128, 128), 128)
        cot = resid_cot[:, lanes]
        for tap in range(31):
            product = cot * wide[pl.ds(tap, rows), lanes]
            sums[pl.ds(tap, 1), lanes] = jnp.sum(product, axis=0, keepdims=True)

    share = width // 8
    for part in range(8):
        low = part * share // 128 * 128
        high = min(low + 384, width)
        piece = sums[:, low:high]
        shift = part * share - low
        if shift:
            piece = pltpu.roll(piece, high - low - shift, 1)
        out[part] = piece[:, :256]


def tap_sums(resid_cot, rim):
    width = resid_cot.shape[1]
    return pl.pallas_call(
        tap_sums_kernel,
        out_shape=jax.ShapeDtypeStruct((8, 32, 256), jnp.float32),
        scratch_shapes=[
            pltpu.VMEM(rim.shape, jnp.float32),
            pltpu.VMEM((32, width), jnp.float32),
        ],
        compiler_params=pltpu.CompilerParams(vmem_limit_bytes=16 * 2**20),
        name="tap_sums",
    )(resid_cot, rim)


def split_columns_kernel(share, parts, out):
    whole = parts[0]
    for part in range(1, 8):
        whole = whole + parts[part]
    whole = jnp.concatenate([whole, jnp.zeros((32, 128), jnp.float32)], axis=1)
    for part in range(16):
        piece = pltpu.roll(whole, 384 - share * part, 1) if part else whole
        out[part] = piece[:, :128]


def split_columns(parts, share):
    return pl.pallas_call(
        lambda *refs: split_columns_kernel(share, *refs),
        out_shape=jax.ShapeDtypeStruct((16, 32, 128), jnp.float32),
        compiler_params=pltpu.CompilerParams(vmem_limit_bytes=16 * 2**20),
        name="split_columns",
    )(parts)


def local(frames, lengths, kernel, expert_ids, gate_weights, w_in, w_out, cotangent):
    block_len = frames.shape[1]
    model_width = frames.shape[2]
    tap_count = kernel.shape[0]
    half_width = tap_count // 2
    place = lax.axis_index("expert")
    my_z, my_y, my_core = place // 8, (place // 2) % 4, place % 2
    positions = place * block_len + jnp.arange(block_len, dtype=jnp.int32)
    frame_mask = (positions < lengths[0]).astype(jnp.float32)
    arrange = order()

    ids = expert_ids[0]
    experts = jnp.arange(16, dtype=jnp.int32)
    named = (ids[:, :, None] == experts).astype(jnp.float32)
    both = named[:, 0] + named[:, 1]
    earlier = jnp.cumsum(both, axis=0) - both
    base = (
        ((experts // 2 - my_y) % 4) * 72
        + (experts // 8 != my_z) * 36
        + (experts % 2 != my_core) * 18
    ).astype(jnp.float32)
    target = jnp.sum(named * (earlier + base)[:, None, :], axis=2).astype(jnp.int32)
    rows = jnp.arange(16 * SLOTS, dtype=jnp.int32)
    hit = rows[:, None, None] == target[None]
    frame_place = jnp.any(hit, axis=2).astype(jnp.bfloat16)
    coeff = 0.5 * gate_weights[0] * frame_mask[:, None]
    row_coeff = jnp.sum(jnp.where(hit, coeff[None], 0.0), axis=(1, 2))

    cot_rows = (row_coeff[:, None] * dot(frame_place, cotangent[0], 1, 0)).astype(jnp.bfloat16)
    masked = (frames[0].astype(jnp.float32) * frame_mask[:, None]).astype(jnp.bfloat16)
    frame_rim = extended(masked, half_width)
    rim = jnp.concatenate([frame_rim, jnp.zeros((2, model_width), jnp.bfloat16)], axis=0)
    conv = jnp.zeros((block_len, model_width), jnp.float32)
    for tap in range(tap_count):
        conv = conv + kernel[tap] * frame_rim[tap : tap + block_len].astype(jnp.float32)
    resid = frames[0].astype(jnp.float32) + conv
    normed_exact, norm_back = jax.vjp(rms_scale, resid)
    normed = normed_exact.astype(jnp.bfloat16)
    normed_rows = dot(frame_place, normed, 1, 0, jnp.bfloat16)

    y_cot = along_y(cot_rows)
    *y_cot, normed_rows = together(*y_cot, normed_rows)
    same_cot, other_cot = to_cores(y_cot, arrange)
    up, down, s1, s3, same_cot, normed_rows = together(
        *neighbours(same_cot, other_cot), same_cot, normed_rows
    )
    gathered_cot = gathered(up, down)
    first_cot = jnp.concatenate([s1, s3], axis=0)
    weight_in = w_in[0]
    weight_out = w_out[0]
    s2, first_far, same_cot, *y_normed = together(
        moved(s1, dx=1), moved(first_cot, dz=2), same_cot, *along_y(normed_rows)
    )
    same, other = to_cores(y_normed, arrange)
    second_cot = jnp.concatenate([same_cot, s2], axis=0)
    first_cot = jnp.concatenate([first_cot, first_far], axis=0)
    first_hidden_cot = dot(first_cot, weight_out, 1, 1)
    up, down, s1, s3 = neighbours(same, other)
    up, down, second_cot, first_hidden_cot = together(up, down, second_cot, first_hidden_cot)
    other_normed = gathered(up, down)
    second_far, s1, s3, same = together(moved(second_cot, dz=2), s1, s3, same)
    gathered_hidden_cot = dot(gathered_cot, weight_out, 1, 1)
    second_cot = jnp.concatenate([second_cot, second_far], axis=0)
    second_hidden_cot = dot(second_cot, weight_out, 1, 1)
    far1, far3, s2, same, second_hidden_cot, gathered_hidden_cot = together(
        moved(s1, dz=2),
        moved(s3, dz=2),
        moved(s3, dx=-1),
        same,
        second_hidden_cot,
        gathered_hidden_cot,
    )
    first_normed = jnp.concatenate([s1, s3, far1, far3], axis=0)
    far, far2 = moved(same, dz=2), moved(s2, dz=2)

    def expert(rows_normed, hidden_cot):
        pre_act = dot(rows_normed, weight_in, 1, 0)
        sigmoid_pre = jax.nn.sigmoid(pre_act)
        hidden = (pre_act * sigmoid_pre).astype(jnp.bfloat16)
        pre_cot = (hidden_cot * sigmoid_pre * (1.0 + pre_act * (1.0 - sigmoid_pre))).astype(
            jnp.bfloat16
        )
        return hidden, pre_cot, dot(pre_cot, weight_in, 1, 1, jnp.bfloat16)

    half = 8 * SLOTS * 2
    other_hidden, other_pre_cot, other_part = expert(other_normed, gathered_hidden_cot)
    first_normed, far, far2, _ = together(first_normed, far, far2, other_part)
    first_hidden, first_pre_cot, first_part = expert(first_normed, first_hidden_cot)
    first_back = moved(first_part[half:], dz=2)
    second_normed = jnp.concatenate([same, s2, far, far2], axis=0)
    second_normed = after(second_normed, first_part)
    second_hidden, second_pre_cot, second_part = expert(second_normed, second_hidden_cot)
    first_back = after(first_back, second_part)
    first_sum = total(first_part[:half], first_back)
    second_sum = total(second_part[:half], moved(second_part[half:], dz=2))

    other_hidden, other_pre_cot, second_part = together(other_hidden, other_pre_cot, second_part)
    grad_out = dot(other_hidden, gathered_cot, 0, 0)
    grad_in = dot(other_normed, other_pre_cot, 0, 0)
    first_hidden, second_hidden, first_cot, second_part = together(
        first_hidden, second_hidden, first_cot, second_part
    )
    cots = jnp.concatenate([first_cot, second_cot], axis=0)
    hiddens = jnp.concatenate([first_hidden, second_hidden], axis=0)
    grad_out = grad_out + dot(hiddens, cots, 0, 0)
    other_part = lax.psum_scatter(
        other_part, "dp", scatter_dimension=0, tiled=True, axis_index_groups=X_GROUPS
    )
    first_pre_cot, second_pre_cot, first_normed, first_sum = together(
        first_pre_cot, second_pre_cot, first_normed, first_sum
    )
    pre_cots = jnp.concatenate([first_pre_cot, second_pre_cot], axis=0)
    normeds = jnp.concatenate([first_normed, second_normed], axis=0)
    grad_in = grad_in + dot(normeds, pre_cots, 0, 0)
    returned, grad_in, grad_out = sent_back(
        first_sum, other_part, second_sum, arrange, grad_in, grad_out
    )
    normed_cot = dot(frame_place, returned, 0, 0)

    resid_cot = cotangent[0].astype(jnp.float32) + norm_back(normed_cot)[0]
    taps = tap_sums(resid_cot, rim)
    taps = split_columns(lax.all_to_all(taps, "dp", 0, 0, tiled=True), model_width // 128)
    taps = lax.all_to_all(taps, "expert", 0, 0, tiled=True)
    grad_kernel = taps[:, :tap_count, : model_width // 128].sum(axis=0)
    grad_rim = extended(resid_cot, half_width)
    spread_back = jnp.zeros((block_len, model_width), jnp.float32)
    for tap in range(tap_count):
        offset = 2 * half_width - tap
        spread_back = spread_back + kernel[tap] * grad_rim[offset : offset + block_len]
    grad_frames = (resid_cot + frame_mask[:, None] * spread_back).astype(jnp.bfloat16)
    return (grad_frames[None], grad_kernel, grad_in[None], grad_out[None])


def solution(mesh):
    return jax.shard_map(
        local,
        mesh=mesh,
        in_specs=(
            P("dp", "expert", None),
            P("dp"),
            P(),
            P("dp", "expert", None),
            P("dp", "expert", None),
            P("expert", None, "dp"),
            P("expert", "dp", None),
            P("dp", "expert", None),
        ),
        out_specs=(
            P("dp", "expert", None),
            P(None, ("dp", "expert")),
            P("expert", None, "dp"),
            P("expert", "dp", None),
        ),
        check_vma=False,
    )
```

```python
import jax
import jax.numpy as jnp
from jax import lax
from jax.experimental import pallas as pl
from jax.experimental.pallas import tpu as pltpu
from jax.sharding import PartitionSpec as P

EPSILON = 1e-06
AXES = ("dp", "expert")
SLOTS = 18
X, Y, Z = 4, 4, 4


def number_of(x, y, z, core):
    return ((z // 2) * X + x) * 16 + (z % 2) * 8 + y * 2 + core


def moved(rows, dx=0, dy=0, dz=0, dc=0):
    pairs = []
    for x in range(X):
        for y in range(Y):
            for z in range(Z):
                for core in range(2):
                    pairs.append(
                        (
                            number_of(x, y, z, core),
                            number_of((x + dx) % X, (y + dy) % Y, (z + dz) % Z, core ^ dc),
                        )
                    )
    return lax.ppermute(rows, AXES, pairs)


def extended(cells, width):
    count = lax.axis_size("expert")
    ends = count - 1
    head = cells[:width]
    tail = cells[-width:]
    return jnp.concatenate(
        [
            lax.ppermute(tail, "expert", [(i, i + 1) for i in range(ends)]),
            cells,
            lax.ppermute(head, "expert", [(i + 1, i) for i in range(ends)]),
        ],
        axis=0,
    )


def rms_scale(values):
    return values * lax.rsqrt(jnp.mean(values * values, axis=-1, keepdims=True) + EPSILON)


def dot(a, b, ca, cb, kind=jnp.float32):
    return lax.dot_general(
        a, b, (((ca,), (cb,)), ((), ())), preferred_element_type=jnp.float32
    ).astype(kind)


def order():
    place = jnp.arange(16 * SLOTS, dtype=jnp.int32)
    slot = place % SLOTS
    source = (place // SLOTS) % 4
    rz = (place // (4 * SLOTS)) % 2
    rc = place // (8 * SLOTS)
    taken = source * 4 * SLOTS + rz * 2 * SLOTS + rc * SLOTS + slot
    return (taken[:, None] == place[None, :]).astype(jnp.bfloat16)


X_GROUPS = [[0, 1, 2, 3], [4, 5, 6, 7]]


def after(value, *earlier):
    return lax.optimization_barrier((value, *earlier))[0]


def together(*values):
    return lax.optimization_barrier(values)


def along_y(rows):
    part = 4 * SLOTS
    pieces = [rows[part * r : part * r + part] for r in range(4)]
    return pieces[:1] + [moved(pieces[r], dy=r) for r in range(1, 4)]


def to_cores(pieces, arrange):
    part = 4 * SLOTS
    placed = dot(arrange, jnp.concatenate(pieces, axis=0), 1, 0, jnp.bfloat16)
    core = moved(placed[2 * part :], dc=1)
    same = jnp.concatenate([placed[:part], core[:part]], axis=0)
    other = jnp.concatenate([placed[part : 2 * part], core[part:]], axis=0)
    return same, other


def neighbours(same, other):
    return moved(other, dz=1), moved(other, dz=-1), moved(same, dx=1), moved(same, dx=-1)


def gathered(up, down):
    other = jnp.concatenate([up, down], axis=0)
    return lax.all_gather(other, "dp", axis=0, tiled=True, axis_index_groups=X_GROUPS)


def total(*terms):
    out = terms[0].astype(jnp.float32)
    for term in terms[1:]:
        out = out + term.astype(jnp.float32)
    return out.astype(jnp.bfloat16)


def sent_back(first, other, second, arrange, grad_in, grad_out):
    part = 4 * SLOTS
    s1, s3, s2, up, down = together(
        moved(first[: 2 * part], dx=-1),
        moved(first[2 * part :], dx=1),
        moved(second[2 * part :], dx=2),
        moved(other[: 2 * part], dz=-1),
        moved(other[2 * part :], dz=1),
    )
    same = total(second[: 2 * part], s1, s3, s2)
    other = total(up, down)
    same, other, grad_in, grad_out = together(same, other, grad_in, grad_out)
    core = moved(jnp.concatenate([same[part:], other[part:]], axis=0), dc=1)
    placed = jnp.concatenate([same[:part], other[:part], core], axis=0)
    rows = dot(arrange, placed, 0, 0, jnp.bfloat16)
    pieces = [rows[part * r : part * r + part] for r in range(4)]
    pieces = pieces[:1] + [moved(pieces[r], dy=-r) for r in range(1, 4)]
    return jnp.concatenate(pieces, axis=0), grad_in, grad_out


def tap_sums_kernel(resid_cot, rim, out, wide, sums):
    rows, width = resid_cot.shape
    wide[...] = rim[...].astype(jnp.float32)
    sums[...] = jnp.zeros_like(sums)

    @pl.loop(0, width // 128)
    def _(tile):
        lanes = pl.ds(pl.multiple_of(tile * 128, 128), 128)
        cot = resid_cot[:, lanes]
        for tap in range(31):
            product = cot * wide[pl.ds(tap, rows), lanes]
            sums[pl.ds(tap, 1), lanes] = jnp.sum(product, axis=0, keepdims=True)

    share = width // 8
    for part in range(8):
        low = part * share // 128 * 128
        high = min(low + 384, width)
        piece = sums[:, low:high]
        shift = part * share - low
        if shift:
            piece = pltpu.roll(piece, high - low - shift, 1)
        out[part] = piece[:, :256]


def tap_sums(resid_cot, rim):
    width = resid_cot.shape[1]
    return pl.pallas_call(
        tap_sums_kernel,
        out_shape=jax.ShapeDtypeStruct((8, 32, 256), jnp.float32),
        scratch_shapes=[
            pltpu.VMEM(rim.shape, jnp.float32),
            pltpu.VMEM((32, width), jnp.float32),
        ],
        compiler_params=pltpu.CompilerParams(vmem_limit_bytes=16 * 2**20),
        name="tap_sums",
    )(resid_cot, rim)


def split_columns_kernel(share, parts, out):
    whole = parts[0]
    for part in range(1, 8):
        whole = whole + parts[part]
    whole = jnp.concatenate([whole, jnp.zeros((32, 128), jnp.float32)], axis=1)
    for part in range(16):
        piece = pltpu.roll(whole, 384 - share * part, 1) if part else whole
        out[part] = piece[:, :128]


def split_columns(parts, share):
    return pl.pallas_call(
        lambda *refs: split_columns_kernel(share, *refs),
        out_shape=jax.ShapeDtypeStruct((16, 32, 128), jnp.float32),
        compiler_params=pltpu.CompilerParams(vmem_limit_bytes=16 * 2**20),
        name="split_columns",
    )(parts)


def local(frames, lengths, kernel, expert_ids, gate_weights, w_in, w_out, cotangent):
    block_len = frames.shape[1]
    model_width = frames.shape[2]
    tap_count = kernel.shape[0]
    half_width = tap_count // 2
    place = lax.axis_index("expert")
    my_z, my_y, my_core = place // 8, (place // 2) % 4, place % 2
    positions = place * block_len + jnp.arange(block_len, dtype=jnp.int32)
    frame_mask = (positions < lengths[0]).astype(jnp.float32)
    arrange = order()

    ids = expert_ids[0]
    experts = jnp.arange(16, dtype=jnp.int32)
    named = (ids[:, :, None] == experts).astype(jnp.float32)
    both = named[:, 0] + named[:, 1]
    earlier = jnp.cumsum(both, axis=0) - both
    base = (
        ((experts // 2 - my_y) % 4) * 72
        + (experts // 8 != my_z) * 36
        + (experts % 2 != my_core) * 18
    ).astype(jnp.float32)
    target = jnp.sum(named * (earlier + base)[:, None, :], axis=2).astype(jnp.int32)
    rows = jnp.arange(16 * SLOTS, dtype=jnp.int32)
    hit = rows[:, None, None] == target[None]
    frame_place = jnp.any(hit, axis=2).astype(jnp.bfloat16)
    coeff = 0.5 * gate_weights[0] * frame_mask[:, None]
    row_coeff = jnp.sum(jnp.where(hit, coeff[None], 0.0), axis=(1, 2))

    cot_rows = (row_coeff[:, None] * dot(frame_place, cotangent[0], 1, 0)).astype(jnp.bfloat16)
    masked = (frames[0].astype(jnp.float32) * frame_mask[:, None]).astype(jnp.bfloat16)
    frame_rim = extended(masked, half_width)
    rim = jnp.concatenate([frame_rim, jnp.zeros((2, model_width), jnp.bfloat16)], axis=0)
    conv = jnp.zeros((block_len, model_width), jnp.float32)
    for tap in range(tap_count):
        conv = conv + kernel[tap] * frame_rim[tap : tap + block_len].astype(jnp.float32)
    resid = frames[0].astype(jnp.float32) + conv
    normed_exact, norm_back = jax.vjp(rms_scale, resid)
    normed = normed_exact.astype(jnp.bfloat16)
    normed_rows = dot(frame_place, normed, 1, 0, jnp.bfloat16)

    y_cot = along_y(cot_rows)
    *y_cot, normed_rows = together(*y_cot, normed_rows)
    same_cot, other_cot = to_cores(y_cot, arrange)
    up, down, s1, s3, same_cot, normed_rows = together(
        *neighbours(same_cot, other_cot), same_cot, normed_rows
    )
    gathered_cot = gathered(up, down)
    first_cot = jnp.concatenate([s1, s3], axis=0)
    weight_in = w_in[0]
    weight_out = w_out[0]
    s2, first_far, same_cot, *y_normed = together(
        moved(s1, dx=1), moved(first_cot, dz=2), same_cot, *along_y(normed_rows)
    )
    same, other = to_cores(y_normed, arrange)
    second_cot = jnp.concatenate([same_cot, s2], axis=0)
    first_cot = jnp.concatenate([first_cot, first_far], axis=0)
    first_hidden_cot = dot(first_cot, weight_out, 1, 1)
    up, down, s1, s3 = neighbours(same, other)
    up, down, second_cot, first_hidden_cot = together(up, down, second_cot, first_hidden_cot)
    other_normed = gathered(up, down)
    second_far, s1, s3, same = together(moved(second_cot, dz=2), s1, s3, same)
    gathered_hidden_cot = dot(gathered_cot, weight_out, 1, 1)
    second_cot = jnp.concatenate([second_cot, second_far], axis=0)
    second_hidden_cot = dot(second_cot, weight_out, 1, 1)
    far1, far3, s2, same, second_hidden_cot, gathered_hidden_cot = together(
        moved(s1, dz=2),
        moved(s3, dz=2),
        moved(s3, dx=-1),
        same,
        second_hidden_cot,
        gathered_hidden_cot,
    )
    first_normed = jnp.concatenate([s1, s3, far1, far3], axis=0)
    far, far2 = moved(same, dz=2), moved(s2, dz=2)

    def expert(rows_normed, hidden_cot):
        pre_act = dot(rows_normed, weight_in, 1, 0)
        sigmoid_pre = jax.nn.sigmoid(pre_act)
        hidden = (pre_act * sigmoid_pre).astype(jnp.bfloat16)
        pre_cot = (hidden_cot * sigmoid_pre * (1.0 + pre_act * (1.0 - sigmoid_pre))).astype(
            jnp.bfloat16
        )
        return hidden, pre_cot, dot(pre_cot, weight_in, 1, 1, jnp.bfloat16)

    half = 8 * SLOTS * 2
    other_hidden, other_pre_cot, other_part = expert(other_normed, gathered_hidden_cot)
    first_normed, far, far2, _ = together(first_normed, far, far2, other_part)
    first_hidden, first_pre_cot, first_part = expert(first_normed, first_hidden_cot)
    first_back = moved(first_part[half:], dz=2)
    second_normed = jnp.concatenate([same, s2, far, far2], axis=0)
    second_normed = after(second_normed, first_part)
    second_hidden, second_pre_cot, second_part = expert(second_normed, second_hidden_cot)
    first_back = after(first_back, second_part)
    first_sum = total(first_part[:half], first_back)
    second_sum = total(second_part[:half], moved(second_part[half:], dz=2))

    other_hidden, other_pre_cot, second_part = together(other_hidden, other_pre_cot, second_part)
    grad_out = dot(other_hidden, gathered_cot, 0, 0)
    grad_in = dot(other_normed, other_pre_cot, 0, 0)
    first_hidden, second_hidden, first_cot, second_part = together(
        first_hidden, second_hidden, first_cot, second_part
    )
    cots = jnp.concatenate([first_cot, second_cot], axis=0)
    hiddens = jnp.concatenate([first_hidden, second_hidden], axis=0)
    grad_out = grad_out + dot(hiddens, cots, 0, 0)
    other_part = lax.psum_scatter(
        other_part, "dp", scatter_dimension=0, tiled=True, axis_index_groups=X_GROUPS
    )
    first_pre_cot, second_pre_cot, first_normed, first_sum = together(
        first_pre_cot, second_pre_cot, first_normed, first_sum
    )
    pre_cots = jnp.concatenate([first_pre_cot, second_pre_cot], axis=0)
    normeds = jnp.concatenate([first_normed, second_normed], axis=0)
    pre_cots, normeds, other_part = together(pre_cots, normeds, other_part)
    grad_in = grad_in + dot(normeds, pre_cots, 0, 0)
    returned, grad_in, grad_out = sent_back(
        first_sum, other_part, second_sum, arrange, grad_in, grad_out
    )
    normed_cot = dot(frame_place, returned, 0, 0)

    resid_cot = cotangent[0].astype(jnp.float32) + norm_back(normed_cot)[0]
    taps = tap_sums(resid_cot, rim)
    taps = split_columns(lax.all_to_all(taps, "dp", 0, 0, tiled=True), model_width // 128)
    taps = lax.all_to_all(taps, "expert", 0, 0, tiled=True)
    grad_kernel = taps[:, :tap_count, : model_width // 128].sum(axis=0)
    grad_rim = extended(resid_cot, half_width)
    spread_back = jnp.zeros((block_len, model_width), jnp.float32)
    for tap in range(tap_count):
        offset = 2 * half_width - tap
        spread_back = spread_back + kernel[tap] * grad_rim[offset : offset + block_len]
    grad_frames = (resid_cot + frame_mask[:, None] * spread_back).astype(jnp.bfloat16)
    return (grad_frames[None], grad_kernel, grad_in[None], grad_out[None])


def solution(mesh):
    return jax.shard_map(
        local,
        mesh=mesh,
        in_specs=(
            P("dp", "expert", None),
            P("dp"),
            P(),
            P("dp", "expert", None),
            P("dp", "expert", None),
            P("expert", None, "dp"),
            P("expert", "dp", None),
            P("dp", "expert", None),
        ),
        out_specs=(
            P("dp", "expert", None),
            P(None, ("dp", "expert")),
            P("expert", None, "dp"),
            P("expert", "dp", None),
        ),
        check_vma=False,
    )
```
